768 devices in a mesh: node: 48 (over x, z), feat: 16 (over y, core).
Axes of the slice: x: 4, y: 8, z: 12, core: 2. Of those that a mesh axis runs over, the one named last changes fastest.
Arguments:
- features: bfloat16 [196608, 768], P('node', 'feat'), may hold values from -6 to 6
- req_local: int32 [48, 48, 256], P('node'), may hold values from 0 to 4095
- nbr_slot: int32 [24576, 25], P('node'), may hold values from 0 to 12287
- target_ids: int32 [24576], P('node'), may hold values from 0 to 4095
- w_self: bfloat16 [768, 1024], replicated, may hold values from -0.21875 to 0.21875
- w_neigh: bfloat16 [768, 1024], replicated, may hold values from -0.875 to 0.875
- bias_one: float32 [1024], P('feat'), may hold values from -3 to 3
- w_two: bfloat16 [1024, 1024], P(None, 'feat'), may hold values from -0.25 to 0.25
- bias_two: float32 [1024], P('feat'), may hold values from -3 to 3
Outputs:
- second_out: bfloat16 [24576, 1024], P('node', 'feat')
The draws below stay inside these ranges and needn't reach their ends.
All inputs are finite; a program needn't handle non-finite values.
Results may differ from the reference program's by a relative error of at most 0.0052.
Values may be sent and summed in bfloat16 or wider, within the bound.
A program may use at most 64 MiB of HBM per device.

```python
import math
import jax
import jax.numpy as jnp
import numpy as np
from jax import lax

D_IN = 768
HIDDEN_SIZE = 1024
NODE_DEV = 4096
TGT_DEV = 512
CAP = 256
FAN = 25
NODES = 196608
TARGETS = 24576
N_NODE = 48


def plant(drawn, own_key, least, largest):
    extent = drawn.shape
    spot = [jax.random.randint(jax.random.fold_in(own_key, axis), (), 0, extent[axis]) for axis in range(len(extent))]
    drawn = drawn.at[tuple(spot)].set(least)
    longest = extent.index(max(extent))
    spot[longest] = (spot[longest] + 1) % extent[longest]
    return drawn.at[tuple(spot)].set(largest)


def block_levels(stream_key, shape, split, smallest, largest):
    def one(position, parts):
        steps = jax.random.uniform(jax.random.fold_in(jax.random.fold_in(stream_key, 6), position), (parts,), jnp.float32, smallest / len(split), largest / len(split))
        return jnp.repeat(jnp.exp(steps), shape[position] // parts).reshape((-1,) + (1,) * (len(shape) - position - 1))

    loudness = one(*split[0])
    for cut in split[1:]:
        loudness = loudness * one(*cut)
    return loudness


def cumulative_ranks(count, skew):
    portions = [(1 << 20) // math.isqrt(standing ** skew) + 1 for standing in range(1, count + 1)]
    spread = 1 + sum(portions) // (1 << 30)
    return np.cumsum(np.array([max(1, weight // spread) for weight in portions]))


def skewed_ids(key, dims, amount, skew):
    grid = cumulative_ranks(amount, skew)
    ticket = jax.random.randint(jax.random.fold_in(key, 1), dims, 0, int(grid[amount - 1]))
    standing = jnp.searchsorted(jnp.asarray(grid, jnp.int32), ticket, side="right")
    return jax.random.permutation(jax.random.fold_in(key, 2), amount)[standing].astype(jnp.int32)


def normal_values(key, dims, deviation, reach, split=(), kind=jnp.bfloat16):
    level = block_levels(key, dims, split, -0.22, 0.18) if split else 1.0
    values = jax.random.normal(key, dims, jnp.float32) * deviation * level
    return jnp.minimum(jnp.maximum(values, -reach), reach).astype(kind)


def setup_inputs(seed: int = 0) -> dict:
    key_list = jax.random.split(jax.random.key(seed), 10)
    features = normal_values(key_list[0], (NODES, D_IN), 1.0, 6.0, ((0, 48), (1, 16)))
    req_local = plant(jax.random.randint(key_list[1], (N_NODE, N_NODE, CAP), 0, NODE_DEV), jax.random.fold_in(key_list[1], 1), 0, NODE_DEV - 1).astype(jnp.int32)
    nbr_slot = plant(skewed_ids(key_list[2], (TARGETS, FAN), N_NODE * CAP, 1), jax.random.fold_in(key_list[2], 3), 0, (N_NODE * CAP) - 1).astype(jnp.int32)
    target_ids = plant(jax.random.randint(key_list[3], (TARGETS,), 0, NODE_DEV), jax.random.fold_in(key_list[3], 1), 0, NODE_DEV - 1).astype(jnp.int32)
    w_self = normal_values(key_list[4], (D_IN, HIDDEN_SIZE), D_IN ** -0.5, 0.21875)
    w_neigh = normal_values(key_list[5], (D_IN, HIDDEN_SIZE), (D_IN // 16) ** -0.5, 0.875)
    bias_one = normal_values(key_list[6], (HIDDEN_SIZE,), 0.5, 3.0, ((0, 16),), jnp.float32)
    w_two = normal_values(key_list[7], (HIDDEN_SIZE, HIDDEN_SIZE), (HIDDEN_SIZE // 2) ** -0.5, 0.25, ((1, 16),))
    bias_two = normal_values(key_list[8], (HIDDEN_SIZE,), 0.5, 3.0, ((0, 16),), jnp.float32)
    return dict(features=features, req_local=req_local, nbr_slot=nbr_slot, target_ids=target_ids, w_self=w_self, w_neigh=w_neigh, bias_one=bias_one, w_two=w_two, bias_two=bias_two)


def reference(features, req_local, nbr_slot, target_ids, w_self, w_neigh, bias_one, w_two, bias_two):
    owners = jnp.arange(N_NODE, dtype=jnp.int32)

    def one_part(part):
        wanted = req_local[part]
        index = (owners[:, None] * NODE_DEV + wanted).reshape(-1).astype(jnp.int32)
        buffer = features[index]
        slots = lax.dynamic_slice_in_dim(nbr_slot, (part * TGT_DEV).astype(jnp.int32), TGT_DEV, 0)
        picked = buffer[slots].astype(jnp.float32)
        neigh_mean = (jnp.sum(picked, axis=1) / FAN).astype(jnp.bfloat16)
        local_ids = lax.dynamic_slice_in_dim(target_ids, (part * TGT_DEV).astype(jnp.int32), TGT_DEV, 0)
        own = features[(local_ids + part * NODE_DEV).astype(jnp.int32)]
        pre = jnp.dot(own, w_self, preferred_element_type=jnp.float32)
        pre = pre + jnp.dot(neigh_mean, w_neigh, preferred_element_type=jnp.float32) + bias_one
        hidden_one = jnp.maximum(pre, 0.0).astype(jnp.bfloat16)
        result = jnp.dot(hidden_one, w_two, preferred_element_type=jnp.float32) + bias_two
        return result.astype(jnp.bfloat16)

    outputs = lax.map(one_part, owners)
    return outputs.reshape(N_NODE * TGT_DEV, HIDDEN_SIZE)
```

```python
import functools

import jax
import jax.numpy as jnp
from jax import lax
from jax.experimental import pallas as pl
from jax.experimental.pallas import tpu as pltpu
from jax.sharding import PartitionSpec as P

FAN = 25
RING_X = 4
F32 = jnp.float32
BF16 = jnp.bfloat16
NT = (((1,), (1,)), ((), ()))
TN = (((0,), (0,)), ((), ()))


def offset(k, ring_x, ring_z):
    pair, side = lax.div(k, 2), lax.rem(k, 2)
    along, dx = lax.div(pair, ring_x), lax.rem(pair, ring_x)
    dz = along + side * (ring_z - 1 - 2 * along)
    return dx, dz


def kernel(
    sizes,
    feat_ref, req_ref, nbr_ref, tgt_ref, ws_ref, wn_ref, b1_ref, w2_ref, b2_ref,
    out_ref,
    table, req_out, req_in, rows_out, rows_in, count, hi_all, lo_all, acc, mixed,
    weight, w2_all, bias_out, bias_in, x_in, y_out, y_in,
    req_ss, req_rs, row_ss, row_rs, w_sem, w2_ss, w2_rs, b_ss, b_rs, x_ss, x_rs, y_ss, y_rs,
):
    ring_x, ring_z, groups, cap, own_rows, targets, cols = sizes
    nodes = ring_x * ring_z
    blocks = own_rows // 256
    share = targets // groups
    hidden = groups * 64
    node, feat = lax.axis_index("node"), lax.axis_index("feat")
    my_x, my_z = lax.div(node, ring_z), lax.rem(node, ring_z)

    def ahead(k):
        dx, dz = offset(k, ring_x, ring_z)
        return lax.rem(my_x + dx, ring_x) * ring_z + lax.rem(my_z + dz, ring_z)

    def behind(k):
        dx, dz = offset(k, ring_x, ring_z)
        return lax.rem(my_x + ring_x - dx, ring_x) * ring_z + lax.rem(my_z + ring_z - dz, ring_z)

    def mate(k):
        return lax.rem(feat + k, groups)

    def node_copy(src, dst, ss, rs, peer):
        return pltpu.make_async_remote_copy(
            src_ref=src, dst_ref=dst, send_sem=ss, recv_sem=rs,
            device_id={"node": peer}, device_id_type=pl.DeviceIdType.MESH,
        )

    def feat_copy(src, dst, ss, rs, peer):
        return pltpu.make_async_remote_copy(
            src_ref=src, dst_ref=dst, send_sem=ss, recv_sem=rs,
            device_id={"feat": peer}, device_id_type=pl.DeviceIdType.MESH,
        )

    def loop(low, high, body):
        def step(k, carry):
            body(k)
            return carry

        lax.fori_loop(low, high, step, 0)

    barrier = pltpu.get_barrier_semaphore()
    loop(1, nodes, lambda k: pl.semaphore_signal(
        barrier, inc=1, device_id={"node": ahead(k)}, device_id_type=pl.DeviceIdType.MESH))
    loop(1, groups, lambda k: pl.semaphore_signal(
        barrier, inc=1, device_id={"feat": mate(k)}, device_id_type=pl.DeviceIdType.MESH))

    def weight_copies(j):
        src = pl.ds(pl.multiple_of(j * cols, cols), cols)
        yield pltpu.make_async_copy(wn_ref.at[src], weight.at[j, pl.ds(0, cols)], w_sem.at[j])
        yield pltpu.make_async_copy(ws_ref.at[src], weight.at[j, pl.ds(cols, cols)], w_sem.at[groups + j])

    for j in range(groups):
        for copy in weight_copies(j):
            copy.start()
    weight[:, pl.ds(2 * cols, 128 - 2 * cols), :] = jnp.zeros((groups, 128 - 2 * cols, hidden), BF16)

    for j in range(blocks):
        table[pl.ds(j * cols, cols), :] = feat_ref[:, pl.ds(j * 256, 256)]
    for j in range(nodes):
        req_out[j] = req_ref[pl.ds(j, 1), :]
    bias_out[...] = jnp.zeros_like(bias_out)
    bias_out[pl.ds(0, 1), pl.ds(0, 64)] = b1_ref[...]
    bias_out[pl.ds(1, 1), pl.ds(0, 64)] = b2_ref[...]
    bias_out[...] = bias_out[...] + pltpu.roll(bias_out[...], 64, 1)
    bias_in[feat] = bias_out[...]
    w2_all[feat] = w2_ref[...]
    req_in[node] = req_out[node]

    pl.semaphore_wait(barrier, nodes - 1 + groups - 1)

    def send_request(k):
        peer = behind(k)
        node_copy(req_out.at[peer], req_in.at[node], req_ss.at[peer], req_rs.at[node], peer).start()

    loop(1, nodes, send_request)

    def send_second(k):
        peer = mate(k)
        feat_copy(bias_out, bias_in.at[feat], b_ss.at[peer], b_rs.at[feat], peer).start()
        feat_copy(w2_ref, w2_all.at[feat], w2_ss.at[peer], w2_rs.at[feat], peer).start()

    loop(1, groups, send_second)

    def pick(index):
        block, within = lax.shift_right_logical(index, 8), lax.bitwise_and(index, 255)
        row = lax.broadcasted_iota(jnp.int32, (256, 256), 0)
        one_hot = jnp.where(row == within, 1.0, 0.0).astype(BF16)
        every = jnp.dot(table[...], one_hot, preferred_element_type=F32)
        found = every[0:cols]
        for j in range(1, blocks):
            found = jnp.where(block == j, every[j * cols:(j + 1) * cols], found)
        return found

    for j in range(targets // 256):
        own = pick(tgt_ref[:, pl.ds(j * 256, 256)])
        wide = jnp.concatenate(
            [jnp.zeros((cols, 256), F32), own, jnp.zeros((128 - 2 * cols, 256), F32)], axis=0)
        mixed[pl.ds(j * 256, 256), :] = wide.T.astype(BF16)

    def serve(k):
        peer = ahead(k)
        node_copy(req_out.at[peer], req_in.at[peer], req_ss.at[peer], req_rs.at[peer], peer).wait_recv()
        rows_out[peer] = pick(req_in[peer]).astype(BF16)
        node_copy(rows_out.at[peer], rows_in.at[node], row_ss.at[peer], row_rs.at[node], peer).start()

    rows_in[node] = pick(req_in[node]).astype(BF16)
    loop(1, nodes, serve)

    slots = nbr_ref[...]
    spread = jnp.where(
        lax.bitwise_and(lax.broadcasted_iota(jnp.int32, (FAN, 256), 1), 31)
        == lax.broadcasted_iota(jnp.int32, (FAN, 256), 0), 1.0, 0.0).astype(BF16)
    hi = lax.shift_right_logical(slots, 8).astype(F32).astype(BF16)
    lo = lax.bitwise_and(slots, 255).astype(F32).astype(BF16)
    hi_all[...] = lax.dot_general(hi, spread, TN, preferred_element_type=F32)
    lo_all[...] = lax.dot_general(lo, spread, TN, preferred_element_type=F32)

    def count_eight(first):
        lane = lax.broadcasted_iota(jnp.int32, (8, 256), 1)
        sub = lax.broadcasted_iota(jnp.int32, (8, 256), 0)
        mine = (lax.shift_right_logical(lane, 5) == sub) & (lax.bitwise_and(lane, 31) < FAN)
        part = pl.ds(pl.multiple_of(first, 8), 8)
        his = jnp.where(mine, hi_all[part, :], -1.0)
        los = jnp.sum(jnp.where(mine, lo_all[part, :], 0.0), axis=0, keepdims=True)
        left = jnp.concatenate([jnp.where(his == float(d), 1.0, 0.0) for d in range(nodes)], axis=0)
        row = lax.broadcasted_iota(jnp.int32, (256, 256), 0)
        right = jnp.where(row == los.astype(jnp.int32), 1.0, 0.0)
        both = lax.dot_general(left.astype(BF16), right.astype(BF16), NT, preferred_element_type=F32)
        return both.reshape(nodes, 8, 256)

    def count_sixteen(j):
        first = pl.multiple_of(j * 16, 16)
        both = jnp.concatenate([count_eight(first), count_eight(first + 8)], axis=1)
        count[:, pl.ds(first, 16), :] = both.astype(BF16)

    loop(0, targets // 16, count_sixteen)

    def add_owner(owner):
        acc[...] += lax.dot_general(count[owner], rows_in[owner], NT, preferred_element_type=F32)

    acc[...] = lax.dot_general(count[node], rows_in[node], NT, preferred_element_type=F32)

    def take(k):
        owner = behind(k)
        node_copy(rows_out.at[owner], rows_in.at[owner], row_ss.at[owner], row_rs.at[owner], owner).wait_recv()
        add_owner(owner)

    loop(1, nodes, take)
    mixed[:, pl.ds(0, cols)] = (acc[...] / FAN).astype(BF16)

    def part_of(peer):
        return mixed.at[pl.ds(pl.multiple_of(peer * share, share), share), :]

    def send_mixed(k):
        peer = mate(k)
        feat_copy(part_of(peer), x_in.at[feat], x_ss.at[peer], x_rs.at[feat], peer).start()

    loop(1, groups, send_mixed)
    x_in[feat] = mixed[pl.ds(pl.multiple_of(feat * share, share), share), :]

    def got_second(k):
        peer = mate(k)
        feat_copy(bias_out, bias_in.at[peer], b_ss.at[peer], b_rs.at[peer], peer).wait_recv()
        feat_copy(w2_ref, w2_all.at[peer], w2_ss.at[peer], w2_rs.at[peer], peer).wait_recv()

    loop(1, groups, got_second)
    for j in range(groups):
        for copy in weight_copies(j):
            copy.wait()

    low_half = lax.broadcasted_iota(jnp.int32, (1, 128), 1) < 64
    bias = [
        jnp.concatenate([
            jnp.where(low_half, bias_in[2 * j, pl.ds(r, 1), :], bias_in[2 * j + 1, pl.ds(r, 1), :])
            for j in range(groups // 2)], axis=1)
        for r in range(2)]

    def got_mixed(k):
        peer = mate(k)
        feat_copy(part_of(peer), x_in.at[peer], x_ss.at[peer], x_rs.at[peer], peer).wait_recv()

    loop(1, groups, got_mixed)

    x = jnp.concatenate([x_in[j] for j in range(groups)], axis=1)
    pre = jnp.dot(x, weight[...].reshape(groups * 128, hidden), preferred_element_type=F32) + bias[0]
    one = jnp.maximum(pre, 0.0).astype(BF16)
    two = lax.dot_general(one, w2_all[...].reshape(hidden, hidden), NT, preferred_element_type=F32) + bias[1]
    two = two.astype(BF16)
    for j in range(groups // 2):
        y_out[j] = two[:, j * 128:(j + 1) * 128]

    def send_second_out(k):
        peer = mate(k)
        feat_copy(y_out.at[lax.div(peer, 2)], y_in.at[feat], y_ss.at[peer], y_rs.at[feat], peer).start()

    loop(1, groups, send_second_out)
    y_in[feat] = y_out[lax.div(feat, 2)]

    def got_second_out(k):
        peer = mate(k)
        feat_copy(y_out.at[lax.div(peer, 2)], y_in.at[peer], y_ss.at[peer], y_rs.at[peer], peer).wait_recv()

    loop(1, groups, got_second_out)
    turned = y_in[...].reshape(targets, 128).astype(F32).T
    out_ref[...] = jnp.where(lax.rem(feat, 2) == 0, turned[0:64], turned[64:128]).astype(BF16)

    def node_sent(k):
        peer = ahead(k)
        node_copy(req_out.at[peer], req_in.at[peer], req_ss.at[peer], req_rs.at[peer], peer).wait_send()
        node_copy(rows_out.at[peer], rows_in.at[peer], row_ss.at[peer], row_rs.at[peer], peer).wait_send()

    loop(1, nodes, node_sent)

    def feat_sent(k):
        peer = mate(k)
        feat_copy(bias_out, bias_in.at[peer], b_ss.at[peer], b_rs.at[peer], peer).wait_send()
        feat_copy(w2_ref, w2_all.at[peer], w2_ss.at[peer], w2_rs.at[peer], peer).wait_send()
        feat_copy(part_of(peer), x_in.at[peer], x_ss.at[peer], x_rs.at[peer], peer).wait_send()
        feat_copy(y_out.at[lax.div(peer, 2)], y_in.at[peer], y_ss.at[peer], y_rs.at[peer], peer).wait_send()

    loop(1, groups, feat_sent)


def local(groups, ring_x, features, req_local, nbr_slot, target_ids, w_self, w_neigh, bias_one, w_two, bias_two):
    _, nodes, cap = req_local.shape
    own_rows, cols = features.shape
    targets = nbr_slot.shape[0]
    hidden = w_self.shape[1]
    share = targets // groups
    sizes = (ring_x, nodes // ring_x, groups, cap, own_rows, targets, cols)
    vmem = pl.BlockSpec(memory_space=pltpu.VMEM)
    hbm = pl.BlockSpec(memory_space=pl.ANY)
    dma = pltpu.SemaphoreType.DMA
    out = pl.pallas_call(
        functools.partial(kernel, sizes),
        out_shape=jax.ShapeDtypeStruct((64, targets), BF16),
        in_specs=[vmem, vmem, vmem, vmem, hbm, hbm, vmem, vmem, vmem],
        out_specs=vmem,
        scratch_shapes=[
            pltpu.VMEM((own_rows // 256 * cols, 256), BF16),
            pltpu.VMEM((nodes, 1, cap), jnp.int32),
            pltpu.VMEM((nodes, 1, cap), jnp.int32),
            pltpu.VMEM((nodes, cols, cap), BF16),
            pltpu.VMEM((nodes, cols, cap), BF16),
            pltpu.VMEM((nodes, targets, cap), BF16),
            pltpu.VMEM((targets, 256), F32),
            pltpu.VMEM((targets, 256), F32),
            pltpu.VMEM((targets, cols), F32),
            pltpu.VMEM((targets, 128), BF16),
            pltpu.VMEM((groups, 128, hidden), BF16),
            pltpu.VMEM((groups, 64, hidden), BF16),
            pltpu.VMEM((8, 128), F32),
            pltpu.VMEM((groups, 8, 128), F32),
            pltpu.VMEM((groups, share, 128), BF16),
            pltpu.VMEM((groups // 2, share, 128), BF16),
            pltpu.VMEM((groups, share, 128), BF16),
            dma((nodes,)), dma((nodes,)), dma((nodes,)), dma((nodes,)),
            dma((2 * groups,)),
            dma((groups,)), dma((groups,)), dma((groups,)), dma((groups,)),
            dma((groups,)), dma((groups,)), dma((groups,)), dma((groups,)),
        ],
        compiler_params=pltpu.CompilerParams(
            collective_id=0, has_side_effects=True, vmem_limit_bytes=56 * 1024 * 1024
        ),
    )(
        features.T, req_local[0], nbr_slot.T, target_ids[None, :], w_self, w_neigh,
        bias_one[None, :], w_two.T, bias_two[None, :],
    )
    return out.T


def solution(mesh):
    placed = (
        P("node", "feat"),
        P("node", None, None),
        P("node", None),
        P("node"),
        P(),
        P(),
        P("feat"),
        P(None, "feat"),
        P("feat"),
    )
    return jax.shard_map(
        functools.partial(local, mesh.shape["feat"], RING_X), mesh=mesh, in_specs=placed,
        out_specs=P("node", "feat"), check_vma=False,
    )
```

```python
import functools

import jax
import jax.numpy as jnp
from jax import lax
from jax.experimental import pallas as pl
from jax.experimental.pallas import tpu as pltpu
from jax.sharding import PartitionSpec as P

FAN = 25
UNROLL = 2
RING_X = 4
F32 = jnp.float32
BF16 = jnp.bfloat16
NT = (((1,), (1,)), ((), ()))
TN = (((0,), (0,)), ((), ()))


def lists(ring_z):
    far = (ring_z // 2 - 1) // 2
    return far, ring_z // 2 - 1 - far


def kernel(
    sizes,
    feat_ref, req_ref, nbr_ref, tgt_ref, ws_ref, wn_ref, b1_ref, w2_ref, b2_ref,
    out_ref,
    table, req_out, req_in, far_out, far_in, near_out, near_in, far_count, near_count,
    nbr_in, his, los, far_sum, near_sum, opposite_sum, mixed,
    weight, w2_all, bias_out, bias_in, x_in, y_out, y_in,
    req_ss, req_rs, far_ss, far_rs, near_ss, near_rs, pair_ss, pair_rs, w_sem, w2_ss, w2_rs, on_ss, b_ss, b_rs, x_ss, x_rs, y_ss, y_rs,
):
    ring_x, ring_z, groups, cap, own_rows, targets, cols = sizes
    nodes = ring_x * ring_z
    blocks = own_rows // 256
    share = targets // groups
    hidden = groups * 64
    node, feat = lax.axis_index("node"), lax.axis_index("feat")
    my_x, my_z = lax.div(node, ring_z), lax.rem(node, ring_z)

    half = ring_z // 2
    far_reach, near_reach = lists(ring_z)
    far_steps, near_steps = 2 * far_reach + 1, 2 * near_reach + 1

    def at(dx, dz):
        z = my_z + dz
        z = jnp.where(z < 0, z + ring_z, jnp.where(z >= ring_z, z - ring_z, z))
        return lax.bitwise_and(my_x + ring_x + dx, ring_x - 1) * ring_z + z

    def place(p, steps):
        p = jnp.int32(p)
        step = steps - 1 - lax.shift_right_logical(p, ring_x.bit_length() - 1)
        ahead = lax.shift_right_logical(step + 1, 1)
        return lax.bitwise_and(p, ring_x - 1), jnp.where(lax.bitwise_and(step, 1) == 1, ahead, -ahead)

    opposite = at(0, half)

    def mate(k):
        return lax.bitwise_and(feat + k, groups - 1)

    sibling = feat + 1 - 2 * lax.bitwise_and(feat, 1)

    def same_core(k):
        return lax.bitwise_and(feat + 2 * k, groups - 1)

    def node_copy(src, dst, ss, rs, peer):
        return pltpu.make_async_remote_copy(
            src_ref=src, dst_ref=dst, send_sem=ss, recv_sem=rs,
            device_id={"node": peer}, device_id_type=pl.DeviceIdType.MESH,
        )

    def feat_copy(src, dst, ss, rs, peer):
        return pltpu.make_async_remote_copy(
            src_ref=src, dst_ref=dst, send_sem=ss, recv_sem=rs,
            device_id={"feat": peer}, device_id_type=pl.DeviceIdType.MESH,
        )

    def loop(low, high, body):
        def step(k, carry):
            body(k)
            return carry

        lax.fori_loop(low, high, step, 0)

    barrier = pltpu.get_barrier_semaphore()
    def greet(k):
        peer = node + k
        peer = jnp.where(peer >= nodes, peer - nodes, peer)
        pl.semaphore_signal(barrier, inc=1, device_id={"node": peer}, device_id_type=pl.DeviceIdType.MESH)

    loop(1, nodes, greet)
    loop(1, groups, lambda k: pl.semaphore_signal(
        barrier, inc=1, device_id={"feat": mate(k)}, device_id_type=pl.DeviceIdType.MESH))

    for j in range(nodes):
        req_out[j] = req_ref[pl.ds(j, 1), :]

    pl.semaphore_wait(barrier, nodes - 1 + groups - 1)

    def nbr_copy():
        return node_copy(nbr_ref, nbr_in, pair_ss.at[0], pair_rs.at[0], opposite)

    def sum_copy():
        return node_copy(far_sum, opposite_sum, pair_ss.at[1], pair_rs.at[1], opposite)

    def request_to(peer):
        return node_copy(req_out.at[peer], req_in.at[node], req_ss.at[peer], req_rs.at[node], peer)

    def request_from(peer):
        return node_copy(req_out.at[peer], req_in.at[peer], req_ss.at[peer], req_rs.at[peer], peer)

    def far_owner(p):
        dx, dz = place(p, far_steps)
        return at(-dx, half - dz)

    def near_owner(p):
        dx, dz = place(p, near_steps)
        return at(-dx, -dz)

    far_all, near_all = far_steps * ring_x, near_steps * ring_x
    near_self, far_self = near_all - ring_x, far_all - ring_x
    nbr_copy().start()
    loop(0, far_all, lambda p: request_to(far_owner(p)).start())
    loop(0, near_self, lambda p: request_to(near_owner(p)).start())
    loop(near_self + 1, near_all, lambda p: request_to(near_owner(p)).start())

    def weight_copies(j):
        src = pl.ds(pl.multiple_of(j * cols, cols), cols)
        yield pltpu.make_async_copy(wn_ref.at[src], weight.at[j, pl.ds(0, cols)], w_sem.at[j])
        yield pltpu.make_async_copy(ws_ref.at[src], weight.at[j, pl.ds(cols, cols)], w_sem.at[groups + j])

    for j in range(blocks):
        table[pl.ds(j * cols, cols), :] = feat_ref[:, pl.ds(j * 256, 256)]
    req_in[node] = req_out[node]
    bias_out[...] = jnp.zeros_like(bias_out)
    bias_out[pl.ds(0, 1), pl.ds(0, 64)] = b1_ref[...]
    bias_out[pl.ds(1, 1), pl.ds(0, 64)] = b2_ref[...]
    bias_out[...] = bias_out[...] + pltpu.roll(bias_out[...], 64, 1)

    def second_copy(k):
        peer = same_core(k)
        return feat_copy(w2_ref, w2_all.at[feat], w2_ss.at[peer], w2_rs.at[feat], peer)

    def second_here(k):
        peer = same_core(k)
        return feat_copy(w2_ref, w2_all.at[peer], w2_ss.at[peer], w2_rs.at[peer], peer)

    def second_on(k):
        source = same_core(k)
        return feat_copy(w2_all.at[source], w2_all.at[source], on_ss.at[k], w2_rs.at[source], sibling)

    def second_beside(k):
        source = lax.bitwise_and(sibling + 2 * k, groups - 1)
        return feat_copy(w2_all.at[source], w2_all.at[source], on_ss.at[k], w2_rs.at[source], sibling)

    def bias_copy(k):
        peer = mate(k)
        return feat_copy(bias_out, bias_in.at[feat], b_ss.at[peer], b_rs.at[feat], peer)

    def pick(index):
        block, within = lax.shift_right_logical(index, 8), lax.bitwise_and(index, 255)
        row = lax.broadcasted_iota(jnp.int32, (256, 256), 0)
        one_hot = jnp.where(row == within, 1.0, 0.0).astype(BF16)
        every = jnp.dot(table[...], one_hot, preferred_element_type=F32)
        found = every[0:cols]
        for j in range(1, blocks):
            found = jnp.where(block == j, every[j * cols:(j + 1) * cols], found)
        return found

    def far_copy(p):
        dx, dz = place(p, far_steps)
        return node_copy(far_out.at[p], far_in.at[p], far_ss.at[p], far_rs.at[p], at(dx, dz))

    def near_copy(p):
        dx, dz = place(p, near_steps)
        return node_copy(near_out.at[p], near_in.at[p], near_ss.at[p], near_rs.at[p], at(dx, dz))

    def far_asker(p):
        dx, dz = place(p, far_steps)
        return at(dx, dz + half)

    def near_asker(p):
        dx, dz = place(p, near_steps)
        return at(dx, dz)

    def serve(asker, out, copy, entries):
        askers = [asker(p) for p in entries]
        for peer in askers:
            request_from(peer).wait_recv()
        for p, peer in zip(entries, askers, strict=True):
            out[p] = pick(req_in[peer]).astype(BF16)
        for p in entries:
            copy(p).start()

    loop(0, far_self // 2, lambda k: serve(far_asker, far_out, far_copy, [2 * k, 2 * k + 1]))
    serve(far_asker, far_out, far_copy, range(far_self + 1, far_all))
    loop(1, groups // 2, lambda k: second_copy(k).start())
    loop(1, groups, lambda k: bias_copy(k).start())
    loop(0, near_self // 2, lambda k: serve(near_asker, near_out, near_copy, [2 * k, 2 * k + 1]))
    serve(near_asker, near_out, near_copy, range(near_self + 1, near_all))
    request_from(opposite).wait_recv()
    far_in[far_self] = pick(req_in[opposite]).astype(BF16)
    near_in[near_self] = pick(req_in[node]).astype(BF16)

    spread = jnp.where(
        lax.bitwise_and(lax.broadcasted_iota(jnp.int32, (FAN, 256), 1), 31)
        == lax.broadcasted_iota(jnp.int32, (FAN, 256), 0), 1.0, 0.0).astype(BF16)

    def spread_slots(slots, which):
        hi = lax.shift_right_logical(slots, 8).astype(F32).astype(BF16)
        lo = lax.bitwise_and(slots, 255).astype(F32).astype(BF16)
        his[which] = lax.dot_general(hi, spread, TN, preferred_element_type=F32)
        los[which] = lax.dot_general(lo, spread, TN, preferred_element_type=F32)

    def count_eight(which, owners, first):
        lane = lax.broadcasted_iota(jnp.int32, (8, 256), 1)
        sub = lax.broadcasted_iota(jnp.int32, (8, 256), 0)
        mine = (lax.shift_right_logical(lane, 5) == sub) & (lax.bitwise_and(lane, 31) < FAN)
        part = pl.ds(pl.multiple_of(first, 8), 8)
        hi = jnp.where(mine, his[which, part, :], -1.0)
        lo = jnp.sum(jnp.where(mine, los[which, part, :], 0.0), axis=0, keepdims=True)
        left = jnp.concatenate([jnp.where(hi == owner, 1.0, 0.0) for owner in owners], axis=0)
        row = lax.broadcasted_iota(jnp.int32, (256, 256), 0)
        right = jnp.where(row == lo.astype(jnp.int32), 1.0, 0.0)
        both = lax.dot_general(left.astype(BF16), right.astype(BF16), NT, preferred_element_type=F32)
        return both.reshape(len(owners), 8, 256)

    def count_some(which, count, owners, low, high):
        def body(k):
            for part in range(UNROLL):
                first = pl.multiple_of((k * UNROLL + part) * 16, 16)
                both = [count_eight(which, owners, first + 8 * i) for i in range(2)]
                count[:, pl.ds(first, 16), :] = jnp.concatenate(both, axis=1).astype(BF16)

        loop(low, high, body)

    def list_owners(steps):
        found = []
        for p in range(steps * ring_x):
            dx, dz = place(p, steps)
            found.append(at(-dx, -dz).astype(F32))
        return found

    turns = targets // (16 * UNROLL)
    nbr_copy().wait_recv()
    spread_slots(nbr_in[...], 1)
    count_some(1, far_count, list_owners(far_steps), 0, turns)

    def add_rows(total, count, rows, entries):
        for p in entries:
            total = total + lax.dot_general(rows[p], count[p], NT, preferred_element_type=F32)
        return total

    def take(copy, sums, count, rows, entries):
        for p in entries:
            copy(p).wait_recv()
        sums[...] = add_rows(sums[...], count, rows, entries)

    def take_all(copy, sums, count, rows, own):
        sums[...] = add_rows(jnp.zeros_like(sums), count, rows, [own])
        loop(0, own // ring_x, lambda k: take(
            copy, sums, count, rows, [ring_x * k + j for j in range(ring_x)]))
        take(copy, sums, count, rows, range(own + 1, own + ring_x))

    take_all(far_copy, far_sum, far_count, far_in, far_self)
    sum_copy().start()

    spread_slots(nbr_ref[...], 0)
    count_some(0, near_count, list_owners(near_steps), 0, turns)

    feat_copy(w2_ref, w2_all.at[feat], on_ss.at[0], w2_rs.at[feat], sibling).start()

    def second_forward(k):
        second_here(k).wait_recv()
        second_on(k).start()

    loop(1, groups // 2, second_forward)

    for j in range(targets // 256):
        own = pick(tgt_ref[:, pl.ds(j * 256, 256)])
        wide = jnp.concatenate(
            [jnp.zeros((cols, 256), F32), own, jnp.zeros((128 - 2 * cols, 256), F32)], axis=0)
        mixed[pl.ds(j * 256, 256), :] = wide.T.astype(BF16)

    for j in range(groups):
        for copy in weight_copies(j):
            copy.start()
    weight[:, pl.ds(2 * cols, 128 - 2 * cols), :] = jnp.zeros((groups, 128 - 2 * cols, hidden), BF16)
    bias_in[feat] = bias_out[...]
    w2_all[feat] = w2_ref[...]

    take_all(near_copy, near_sum, near_count, near_in, near_self)
    sum_copy().wait_recv()
    mean = (near_sum[...] + opposite_sum[...]) / FAN
    mean = jnp.concatenate([mean, jnp.zeros((128 - cols, targets), F32)], axis=0)
    mixed[:, pl.ds(0, cols)] = mean.T[:, 0:cols].astype(BF16)

    def part_of(peer):
        return mixed.at[pl.ds(pl.multiple_of(peer * share, share), share), :]

    def send_mixed(k):
        peer = mate(k)
        feat_copy(part_of(peer), x_in.at[feat], x_ss.at[peer], x_rs.at[feat], peer).start()

    loop(1, groups, send_mixed)
    x_in[feat] = mixed[pl.ds(pl.multiple_of(feat * share, share), share), :]

    def bias_here(k):
        peer = mate(k)
        return feat_copy(bias_out, bias_in.at[peer], b_ss.at[peer], b_rs.at[peer], peer)

    loop(1, groups, lambda k: bias_here(k).wait_recv())
    loop(0, groups // 2, lambda k: second_beside(k).wait_recv())

    loop(0, far_all, lambda p: request_to(far_owner(p)).wait_send())
    loop(0, near_self, lambda p: request_to(near_owner(p)).wait_send())
    loop(near_self + 1, near_all, lambda p: request_to(near_owner(p)).wait_send())
    loop(0, far_self, lambda p: far_copy(p).wait_send())
    loop(far_self + 1, far_all, lambda p: far_copy(p).wait_send())
    loop(0, near_self, lambda p: near_copy(p).wait_send())
    loop(near_self + 1, near_all, lambda p: near_copy(p).wait_send())
    nbr_copy().wait_send()
    sum_copy().wait_send()
    loop(1, groups // 2, lambda k: second_copy(k).wait_send())
    loop(0, groups // 2, lambda k: second_on(k).wait_send())
    loop(1, groups, lambda k: bias_copy(k).wait_send())
    for j in range(groups):
        for copy in weight_copies(j):
            copy.wait()

    low_half = lax.broadcasted_iota(jnp.int32, (1, 128), 1) < 64
    bias = [
        jnp.concatenate([
            jnp.where(low_half, bias_in[2 * j, pl.ds(r, 1), :], bias_in[2 * j + 1, pl.ds(r, 1), :])
            for j in range(groups // 2)], axis=1)
        for r in range(2)]

    def got_mixed(k):
        peer = mate(k)
        feat_copy(part_of(peer), x_in.at[peer], x_ss.at[peer], x_rs.at[peer], peer).wait_recv()

    loop(1, groups, got_mixed)

    x = jnp.concatenate([x_in[j] for j in range(groups)], axis=1)
    pre = jnp.dot(x, weight[...].reshape(groups * 128, hidden), preferred_element_type=F32) + bias[0]
    one = jnp.maximum(pre, 0.0).astype(BF16)
    two = lax.dot_general(one, w2_all[...].reshape(hidden, hidden), NT, preferred_element_type=F32) + bias[1]
    two = two.astype(BF16)
    for j in range(groups // 2):
        y_out[j] = two[:, j * 128:(j + 1) * 128]

    def send_second_out(k):
        peer = mate(k)
        feat_copy(y_out.at[lax.div(peer, 2)], y_in.at[feat], y_ss.at[peer], y_rs.at[feat], peer).start()

    loop(1, groups, send_second_out)
    y_in[feat] = y_out[lax.div(feat, 2)]

    def got_second_out(k):
        peer = mate(k)
        feat_copy(y_out.at[lax.div(peer, 2)], y_in.at[peer], y_ss.at[peer], y_rs.at[peer], peer).wait_recv()

    loop(1, groups, got_second_out)
    turned = y_in[...].reshape(targets, 128).astype(F32).T
    out_ref[...] = jnp.where(lax.rem(feat, 2) == 0, turned[0:64], turned[64:128]).astype(BF16)

    def feat_sent(k):
        peer = mate(k)
        feat_copy(part_of(peer), x_in.at[peer], x_ss.at[peer], x_rs.at[peer], peer).wait_send()
        feat_copy(y_out.at[lax.div(peer, 2)], y_in.at[peer], y_ss.at[peer], y_rs.at[peer], peer).wait_send()

    loop(1, groups, feat_sent)


def local(groups, ring_x, features, req_local, nbr_slot, target_ids, w_self, w_neigh, bias_one, w_two, bias_two):
    _, nodes, cap = req_local.shape
    own_rows, cols = features.shape
    targets = nbr_slot.shape[0]
    hidden = w_self.shape[1]
    share = targets // groups
    sizes = (ring_x, nodes // ring_x, groups, cap, own_rows, targets, cols)
    far, near = ((2 * reach + 1) * ring_x for reach in lists(nodes // ring_x))
    vmem = pl.BlockSpec(memory_space=pltpu.VMEM)
    hbm = pl.BlockSpec(memory_space=pl.ANY)
    dma = pltpu.SemaphoreType.DMA
    out = pl.pallas_call(
        functools.partial(kernel, sizes),
        out_shape=jax.ShapeDtypeStruct((64, targets), BF16),
        in_specs=[vmem, vmem, vmem, vmem, hbm, hbm, vmem, vmem, vmem],
        out_specs=vmem,
        scratch_shapes=[
            pltpu.VMEM((own_rows // 256 * cols, 256), BF16),
            pltpu.VMEM((nodes, 1, cap), jnp.int32),
            pltpu.VMEM((nodes, 1, cap), jnp.int32),
            pltpu.VMEM((far, cols, cap), BF16),
            pltpu.VMEM((far, cols, cap), BF16),
            pltpu.VMEM((near, cols, cap), BF16),
            pltpu.VMEM((near, cols, cap), BF16),
            pltpu.VMEM((far, targets, cap), BF16),
            pltpu.VMEM((near, targets, cap), BF16),
            pltpu.VMEM(nbr_slot.shape[::-1], jnp.int32),
            pltpu.VMEM((2, targets, 256), F32),
            pltpu.VMEM((2, targets, 256), F32),
            pltpu.VMEM((cols, targets), F32),
            pltpu.VMEM((cols, targets), F32),
            pltpu.VMEM((cols, targets), F32),
            pltpu.VMEM((targets, 128), BF16),
            pltpu.VMEM((groups, 128, hidden), BF16),
            pltpu.VMEM((groups, 64, hidden), BF16),
            pltpu.VMEM((8, 128), F32),
            pltpu.VMEM((groups, 8, 128), F32),
            pltpu.VMEM((groups, share, 128), BF16),
            pltpu.VMEM((groups // 2, share, 128), BF16),
            pltpu.VMEM((groups, share, 128), BF16),
            dma((nodes,)), dma((nodes,)), dma((far,)), dma((far,)), dma((near,)), dma((near,)), dma((2,)), dma((2,)),
            dma((2 * groups,)),
            dma((groups,)), dma((groups,)), dma((groups // 2,)), dma((groups,)), dma((groups,)),
            dma((groups,)), dma((groups,)), dma((groups,)), dma((groups,)),
        ],
        compiler_params=pltpu.CompilerParams(
            collective_id=0, has_side_effects=True, vmem_limit_bytes=56 * 1024 * 1024
        ),
    )(
        features.T, req_local[0], nbr_slot.T, target_ids[None, :], w_self, w_neigh,
        bias_one[None, :], w_two.T, bias_two[None, :],
    )
    return out.T


def solution(mesh):
    placed = (
        P("node", "feat"),
        P("node", None, None),
        P("node", None),
        P("node"),
        P(),
        P(),
        P("feat"),
        P(None, "feat"),
        P("feat"),
    )
    return jax.shard_map(
        functools.partial(local, mesh.shape["feat"], RING_X), mesh=mesh, in_specs=placed,
        out_specs=P("node", "feat"), check_vma=False,
    )
```

```python
import functools

import jax
import jax.numpy as jnp
from jax import lax
from jax.experimental import pallas as pl
from jax.experimental.pallas import tpu as pltpu
from jax.sharding import PartitionSpec as P

FAN = 25
RING_X = 4
UNROLL = 4
F32 = jnp.float32
BF16 = jnp.bfloat16
PARTIAL = BF16
EARLY = 4
MESH = pl.DeviceIdType.MESH
NT = (((1,), (1,)), ((), ()))
TN = (((0,), (0,)), ((), ()))


def lists(ring_z):
    far = (ring_z // 2 - 1) // 2
    return far, ring_z // 2 - 1 - far


def kernel(
    sizes,
    feat_hbm, req_hbm, nbr_hbm, tgt_hbm, ws_ref, wn_ref, b1_hbm, w2_hbm, b2_hbm,
    out_ref,
    feat_ref, req_ref, nbr_ref, tgt_ref, b1_ref, w2_ref, b2_ref,
    table, req_out, far_req, near_req, far_out, far_in, near_out, near_in, far_count, near_count,
    nbr_in, his, los, far_sum, near_sum, far_send, opposite_sum,
    w_own, w_nbr, w2_all, bias_out, bias_in, own_out, own_in, mean_out, mean_in, pre_own, y_out, y_in,
    req_ss, far_req_rs, near_req_rs, far_ss, far_rs, near_ss, near_rs, pair_ss, pair_rs,
    in_sem, w_sem, up_ss, up_rs, down_ss, down_rs, on_ss, on_rs, group_ss, group_rs,
):
    ring_x, ring_z, groups, own_rows, targets, cols = sizes
    nodes, chips = ring_x * ring_z, groups // 2
    blocks, part = own_rows // 256, targets // groups // 2
    hidden = groups * 64
    node, feat = lax.axis_index("node"), lax.axis_index("feat")
    my_x, my_z = lax.div(node, ring_z), lax.rem(node, ring_z)
    core = lax.bitwise_and(feat, 1)
    chip = lax.shift_right_logical(feat, 1)
    half = ring_z // 2
    far_reach, near_reach = lists(ring_z)
    far_steps, near_steps = 2 * far_reach + 1, 2 * near_reach + 1
    far_all, near_all = far_steps * ring_x, near_steps * ring_x
    far_self, near_self = far_all - ring_x, near_all - ring_x

    def at(dx, dz):
        z = my_z + dz
        z = jnp.where(z < 0, z + ring_z, jnp.where(z >= ring_z, z - ring_z, z))
        return lax.bitwise_and(my_x + ring_x + dx, ring_x - 1) * ring_z + z

    def place(p, steps):
        if isinstance(p, int):
            step = steps - 1 - p // ring_x
            return p % ring_x, (step + 1) // 2 * (1 if step % 2 else -1)
        step = steps - 1 - lax.shift_right_logical(p, ring_x.bit_length() - 1)
        ahead = lax.shift_right_logical(step + 1, 1)
        return lax.bitwise_and(p, ring_x - 1), jnp.where(lax.bitwise_and(step, 1) == 1, ahead, -ahead)

    def mate(k):
        return lax.bitwise_and(feat + k, groups - 1)

    def copy_to(axis, peer, src, dst, ss, rs):
        return pltpu.make_async_remote_copy(
            src_ref=src, dst_ref=dst, send_sem=ss, recv_sem=rs,
            device_id={axis: peer}, device_id_type=MESH,
        )

    def loop(low, high, body):
        def step(k, carry):
            body(k)
            return carry

        lax.fori_loop(low, high, step, 0)

    arrivals = [
        pltpu.make_async_copy(src, dst, in_sem.at[i])
        for i, (src, dst) in enumerate((
            (req_hbm, req_ref), (nbr_hbm, nbr_ref), (feat_hbm, feat_ref), (w2_hbm, w2_ref),
            (tgt_hbm, tgt_ref), (b1_hbm, b1_ref), (b2_hbm, b2_ref)))]
    for copy in arrivals:
        copy.start()

    barrier = pltpu.get_barrier_semaphore()
    for dz in sorted(range(ring_z), key=lambda z: -min(z, ring_z - z)):
        for dx in range(ring_x):
            if dx or dz:
                pl.semaphore_signal(barrier, inc=1, device_id={"node": at(dx, dz)}, device_id_type=MESH)
    for k in range(1, groups):
        pl.semaphore_signal(barrier, inc=1, device_id={"feat": mate(k)}, device_id_type=MESH)

    w_copies = [
        pltpu.make_async_copy(src, dst.at[:, pl.ds(0, cols), :], w_sem.at[i])
        for i, (src, dst) in enumerate(((ws_ref, w_own), (wn_ref, w_nbr)))]
    arrivals[0].wait()
    for j in range(nodes):
        req_out[j] = req_ref[pl.ds(j, 1), :]
    for copy in arrivals[1:]:
        copy.wait()

    pl.semaphore_wait(barrier, nodes - 1 + groups - 1)

    opposite = at(0, half)
    nbr_copy = copy_to("node", opposite, nbr_ref, nbr_in, pair_ss.at[0], pair_rs.at[0])
    sum_copy = copy_to("node", opposite, far_send, opposite_sum, pair_ss.at[1], pair_rs.at[1])
    for p in range(far_all):
        dx, dz = place(p, far_steps)
        owner = at(-dx, half - dz)
        copy_to("node", owner, req_out.at[owner], far_req.at[p], req_ss, far_req_rs.at[p // ring_x]).start()
    nbr_copy.start()
    for p in range(near_all):
        if p != near_self:
            dx, dz = place(p, near_steps)
            owner = at(-dx, -dz)
            copy_to("node", owner, req_out.at[owner], near_req.at[p], req_ss, near_req_rs.at[p // ring_x]).start()
    near_req[near_self] = req_out[node]

    for copy in w_copies:
        copy.start()
    for j in range(blocks):
        table[pl.ds(j * cols, cols), :] = feat_ref[:, pl.ds(j * 256, 256)]
    bias_out[...] = jnp.zeros_like(bias_out)
    bias_out[pl.ds(0, 1), pl.ds(0, 64)] = b1_ref[...]
    bias_out[pl.ds(1, 1), pl.ds(0, 64)] = b2_ref[...]
    bias_out[...] = bias_out[...] + pltpu.roll(bias_out[...], 64, 1)
    bias_in[0] = bias_out[...]

    ups, downs = chips // 2, (chips - 1) // 2

    def up(step):
        slot = w2_all.at[core, lax.bitwise_and(chip - step + chips, chips - 1)]
        return copy_to("feat", mate(2), slot if step else w2_ref, slot, up_ss.at[step], up_rs.at[step])

    def down(step):
        slot = w2_all.at[core, lax.bitwise_and(chip + step, chips - 1)]
        return copy_to("feat", mate(groups - 2), slot if step else w2_ref, slot, down_ss.at[step], down_rs.at[step])

    def pass_on(step):
        for copy, steps in ((up, ups), (down, downs)):
            if 0 < step <= steps:
                copy(step - 1).wait_recv()
            if step < steps:
                copy(step).start()

    w2_all[core, chip] = w2_ref[...]
    pass_on(0)

    def to_mates(src, dst, which):
        for k in sorted(range(1, groups), key=lambda k: -min(k, groups - k)):
            peer = mate(k)
            copy_to("feat", peer, src(peer), dst.at[k], group_ss.at[which], group_rs.at[which]).start()

    def from_mates(dst, which):
        rest = dst.at[pl.ds(1, groups - 1)]
        return copy_to("feat", mate(1), rest, rest, group_ss.at[which], group_rs.at[which])

    spread = jnp.where(
        lax.bitwise_and(lax.broadcasted_iota(jnp.int32, (FAN, 256), 1), 31)
        == lax.broadcasted_iota(jnp.int32, (FAN, 256), 0), 1.0, 0.0).astype(BF16)

    def spread_slots(slots, which):
        hi = lax.shift_right_logical(slots, 8).astype(F32).astype(BF16)
        lo = lax.bitwise_and(slots, 255).astype(F32).astype(BF16)
        his[which] = lax.dot_general(hi, spread, TN, preferred_element_type=F32)
        los[which] = lax.dot_general(lo, spread, TN, preferred_element_type=F32)

    def count_eight(which, owners, first):
        lane = lax.broadcasted_iota(jnp.int32, (8, 256), 1)
        sub = lax.broadcasted_iota(jnp.int32, (8, 256), 0)
        mine = (lax.shift_right_logical(lane, 5) == sub) & (lax.bitwise_and(lane, 31) < FAN)
        rows = pl.ds(pl.multiple_of(first, 8), 8)
        hi = jnp.where(mine, his[which, rows, :], -1.0)
        lo = jnp.sum(jnp.where(mine, los[which, rows, :], 0.0), axis=0, keepdims=True)
        left = jnp.concatenate([jnp.where(hi == owner, 1.0, 0.0) for owner in owners], axis=0)
        row = lax.broadcasted_iota(jnp.int32, (256, 256), 0)
        right = jnp.where(row == lo.astype(jnp.int32), 1.0, 0.0)
        both = lax.dot_general(left.astype(BF16), right.astype(BF16), NT, preferred_element_type=F32)
        return both.reshape(len(owners), 8, 256)

    def count_some(which, count, steps, low, high):
        owners = []
        for p in range(steps * ring_x):
            dx, dz = place(p, steps)
            owners.append(at(-dx, -dz).astype(F32))

        def body(k):
            for turn in range(UNROLL):
                first = pl.multiple_of((k * UNROLL + turn) * 16, 16)
                both = [count_eight(which, owners, first + 8 * i) for i in range(2)]
                count[:, pl.ds(first, 16), :] = jnp.concatenate(both, axis=1).astype(BF16)

        loop(low, high, body)

    turns = targets // (16 * UNROLL)
    early = min(EARLY, turns)
    spread_slots(nbr_ref[...], 0)
    count_some(0, near_count, near_steps, 0, early)

    def pick(index):
        block, within = lax.shift_right_logical(index, 8), lax.bitwise_and(index, 255)
        row = lax.broadcasted_iota(jnp.int32, (256, 256), 0)
        one_hot = jnp.where(row == within, 1.0, 0.0).astype(BF16)
        every = jnp.dot(table[...], one_hot, preferred_element_type=F32)
        found = every[0:cols]
        for j in range(1, blocks):
            found = jnp.where(block == j, every[j * cols:(j + 1) * cols], found)
        return found

    def span(refs, first, size):
        return refs.at[pl.ds(first, size)]

    def arrive(refs, sems, first, size, group):
        rest = span(refs, first, size)
        copy_to("node", opposite, rest, rest, req_ss, sems.at[group]).wait_recv()

    def serve(req, req_rs, out, into, ss, rs, steps, group, entries):
        arrive(req, req_rs, entries[0], len(entries), group)
        for p in entries:
            out[p] = pick(req[p]).astype(BF16)
        for p in entries:
            dx, dz = place(p, steps)
            copy_to("node", at(dx, dz), out.at[p], into.at[p], ss, rs.at[group]).start()

    loop(0, far_steps - 1, lambda g: serve(
        far_req, far_req_rs, far_out, far_in, far_ss, far_rs, far_steps, g,
        [ring_x * g + j for j in range(ring_x)]))
    arrive(far_req, far_req_rs, far_self, ring_x, far_steps - 1)
    for p in range(far_self, far_all):
        found = pick(far_req[p]).astype(BF16)
        if p == far_self:
            far_in[p] = found
        else:
            far_out[p] = found
            dx, dz = place(p, far_steps)
            copy_to("node", at(dx, dz), far_out.at[p], far_in.at[p], far_ss, far_rs.at[far_steps - 1]).start()
    pass_on(1)
    loop(0, near_steps - 1, lambda g: serve(
        near_req, near_req_rs, near_out, near_in, near_ss, near_rs, near_steps, g,
        [ring_x * g + j for j in range(ring_x)]))
    serve(near_req, near_req_rs, near_out, near_in, near_ss, near_rs, near_steps, near_steps - 1,
          list(range(near_self + 1, near_all)))
    near_in[near_self] = pick(near_req[near_self]).astype(BF16)
    pass_on(2)

    nbr_copy.wait_recv()
    spread_slots(nbr_in[...], 1)
    count_some(1, far_count, far_steps, 0, turns)

    def add_rows(total, count, rows, entries):
        for p in entries:
            total = total + lax.dot_general(rows[p], count[p], NT, preferred_element_type=F32)
        return total

    def take(rows, rs, count, sums, group, entries):
        arrive(rows, rs, entries[0], len(entries), group)
        sums[...] = add_rows(sums[...], count, rows, entries)

    def take_all(rows, rs, count, sums, steps):
        own = (steps - 1) * ring_x
        sums[...] = add_rows(jnp.zeros_like(sums), count, rows, [own])
        loop(0, steps - 1, lambda g: take(rows, rs, count, sums, g, [ring_x * g + j for j in range(ring_x)]))
        take(rows, rs, count, sums, steps - 1, list(range(own + 1, own + ring_x)))

    take_all(far_in, far_rs, far_count, far_sum, far_steps)
    far_send[...] = far_sum[...].astype(PARTIAL)
    sum_copy.start()
    pass_on(3)

    def pack(turned):
        gap = jnp.zeros((64 - cols, targets // 2), F32)
        return jnp.concatenate(
            [turned[:, :targets // 2], gap, turned[:, targets // 2:], gap], axis=0).T.astype(BF16)

    def share_of(ref):
        return lambda peer: ref.at[pl.ds(pl.multiple_of(peer * part, part), part), :]

    def unpack(ref):
        tiles = [ref[lax.bitwise_and(feat - j + groups, groups - 1)] for j in range(groups)]
        top = jnp.concatenate(tiles, axis=1)
        rolled = [pltpu.roll(tile.astype(F32), 64, 1).astype(BF16) for tile in tiles]
        return jnp.concatenate([top, jnp.concatenate(rolled, axis=1)], axis=0)

    own = jnp.concatenate([pick(tgt_ref[:, pl.ds(j * 256, 256)]) for j in range(targets // 256)], axis=1)
    own_out[...] = pack(own)
    own_in[0] = own_out[pl.ds(pl.multiple_of(feat * part, part), part), :]
    to_mates(share_of(own_out), own_in, 0)
    to_mates(lambda peer: bias_out, bias_in, 1)

    count_some(0, near_count, near_steps, early, turns)
    take_all(near_in, near_rs, near_count, near_sum, near_steps)

    pass_on(4)
    side = copy_to("feat", feat + 1 - 2 * core, w2_all.at[core], w2_all.at[core], on_ss, on_rs)
    side.start()

    for copy, weight in zip(w_copies, (w_own, w_nbr), strict=True):
        weight[:, pl.ds(cols, 128 - cols), :] = jnp.zeros((groups, 128 - cols, hidden), BF16)
        copy.wait()
    from_mates(own_in, 0).wait_recv()
    from_mates(bias_in, 1).wait_recv()
    low_half = lax.broadcasted_iota(jnp.int32, (1, 128), 1) < 64

    def bias_row(row, order):
        def of(g):
            return bias_in[lax.bitwise_and(feat - g + groups, groups - 1), pl.ds(row, 1), :]

        pairs = zip(order[::2], order[1::2], strict=True)
        return jnp.concatenate([jnp.where(low_half, of(a), of(b)) for a, b in pairs], axis=1)

    by_core = [2 * j + c for c in range(2) for j in range(chips)]
    second_bias = bias_row(1, by_core)
    pre_own[...] = jnp.dot(
        unpack(own_in), w_own[...].reshape(groups * 128, hidden), preferred_element_type=F32,
    ) + bias_row(0, list(range(groups)))

    def sent(refs, size, sem):
        rest = span(refs, 0, size)
        copy_to("node", opposite, rest, rest, sem, pair_rs.at[0]).wait_send()

    sent(req_out, nodes - 1, req_ss)
    sent(far_out, far_all - 1, far_ss)
    sent(near_out, near_all - 1, near_ss)
    nbr_copy.wait_send()
    for copy, steps in ((up, ups), (down, downs)):
        for step in range(steps):
            copy(step).wait_send()
    from_mates(own_in, 0).wait_send()
    from_mates(bias_in, 1).wait_send()

    sum_copy.wait_recv()
    mean_out[...] = pack((near_sum[...] + opposite_sum[...].astype(F32)) / FAN)
    to_mates(share_of(mean_out), mean_in, 2)
    mean_in[0] = mean_out[pl.ds(pl.multiple_of(feat * part, part), part), :]
    sum_copy.wait_send()
    side.wait_send()
    other = w2_all.at[1 - core]
    copy_to("feat", feat + 1 - 2 * core, other, other, on_ss, on_rs).wait_recv()
    from_mates(mean_in, 2).wait_recv()

    pre = pre_own[...] + jnp.dot(
        unpack(mean_in), w_nbr[...].reshape(groups * 128, hidden), preferred_element_type=F32)
    one = jnp.maximum(pre, 0.0).astype(BF16)
    two = lax.dot_general(one, w2_all[...].reshape(hidden, hidden), NT, preferred_element_type=F32) + second_bias
    for j in range(groups // 2):
        above, below = two[:part, j * 128:(j + 1) * 128], two[part:, j * 128:(j + 1) * 128]
        y_out[2 * j] = jnp.where(low_half, above, pltpu.roll(below, 64, 1)).astype(BF16)
        y_out[2 * j + 1] = jnp.where(low_half, pltpu.roll(above, 64, 1), below).astype(BF16)

    def rank(peer):
        return lax.bitwise_and(peer, 1) * chips + lax.shift_right_logical(peer, 1)

    to_mates(lambda peer: y_out.at[rank(peer)], y_in, 3)
    y_in[0] = y_out[rank(feat)]
    from_mates(mean_in, 2).wait_send()
    from_mates(y_in, 3).wait_recv()
    shares = [y_in[lax.bitwise_and(feat - j + groups, groups - 1)] for j in range(groups)]
    turned = jnp.concatenate(shares, axis=0).astype(F32).T
    out_ref[...] = jnp.concatenate([turned[0:64], turned[64:128]], axis=1).astype(BF16)
    from_mates(y_in, 3).wait_send()


def local(groups, ring_x, features, req_local, nbr_slot, target_ids, w_self, w_neigh, bias_one, w_two, bias_two):
    _, nodes, cap = req_local.shape
    own_rows, cols = features.shape
    targets, fan = nbr_slot.shape
    hidden = w_self.shape[1]
    part, chips = targets // groups // 2, groups // 2
    sizes = (ring_x, nodes // ring_x, groups, own_rows, targets, cols)
    far_steps, near_steps = (2 * reach + 1 for reach in lists(nodes // ring_x))
    far, near = far_steps * ring_x, near_steps * ring_x
    vmem = pl.BlockSpec(memory_space=pltpu.VMEM)
    hbm = pl.BlockSpec(memory_space=pl.ANY)
    dma = pltpu.SemaphoreType.DMA
    out = pl.pallas_call(
        functools.partial(kernel, sizes),
        out_shape=jax.ShapeDtypeStruct((64, targets), BF16),
        in_specs=[hbm] * 9,
        out_specs=vmem,
        scratch_shapes=[
            pltpu.VMEM((cols, own_rows), BF16),
            pltpu.VMEM((nodes, cap), jnp.int32),
            pltpu.VMEM((fan, targets), jnp.int32),
            pltpu.VMEM((1, targets), jnp.int32),
            pltpu.VMEM((1, 64), F32),
            pltpu.VMEM((64, hidden), BF16),
            pltpu.VMEM((1, 64), F32),
            pltpu.VMEM((own_rows // 256 * cols, 256), BF16),
            pltpu.VMEM((nodes, 1, cap), jnp.int32),
            pltpu.VMEM((far, 1, cap), jnp.int32),
            pltpu.VMEM((near, 1, cap), jnp.int32),
            pltpu.VMEM((far, cols, cap), BF16),
            pltpu.VMEM((far, cols, cap), BF16),
            pltpu.VMEM((near, cols, cap), BF16),
            pltpu.VMEM((near, cols, cap), BF16),
            pltpu.VMEM((far, targets, cap), BF16),
            pltpu.VMEM((near, targets, cap), BF16),
            pltpu.VMEM((fan, targets), jnp.int32),
            pltpu.VMEM((2, targets, 256), F32),
            pltpu.VMEM((2, targets, 256), F32),
            pltpu.VMEM((cols, targets), F32),
            pltpu.VMEM((cols, targets), F32),
            pltpu.VMEM((cols, targets), PARTIAL),
            pltpu.VMEM((cols, targets), PARTIAL),
            pltpu.VMEM((groups, 128, hidden), BF16),
            pltpu.VMEM((groups, 128, hidden), BF16),
            pltpu.VMEM((2, chips, 64, hidden), BF16),
            pltpu.VMEM((8, 128), F32),
            pltpu.VMEM((groups, 8, 128), F32),
            pltpu.VMEM((targets // 2, 128), BF16),
            pltpu.VMEM((groups, part, 128), BF16),
            pltpu.VMEM((targets // 2, 128), BF16),
            pltpu.VMEM((groups, part, 128), BF16),
            pltpu.VMEM((2 * part, hidden), F32),
            pltpu.VMEM((groups, part, 128), BF16),
            pltpu.VMEM((groups, part, 128), BF16),
            dma(()), dma((far_steps,)), dma((near_steps,)),
            dma(()), dma((far_steps,)), dma(()), dma((near_steps,)), dma((2,)), dma((2,)),
            dma((7,)), dma((2,)), dma((4,)), dma((4,)), dma((4,)), dma((4,)), dma(()), dma(()), dma((4,)), dma((4,)),
        ],
        compiler_params=pltpu.CompilerParams(
            collective_id=0, has_side_effects=True, vmem_limit_bytes=56 * 1024 * 1024
        ),
    )(
        features.T, req_local[0], nbr_slot.T, target_ids[None, :],
        w_self.reshape(groups, cols, hidden), w_neigh.reshape(groups, cols, hidden),
        bias_one[None, :], w_two.T, bias_two[None, :],
    )
    return out.T


def solution(mesh):
    placed = (
        P("node", "feat"),
        P("node", None, None),
        P("node", None),
        P("node"),
        P(),
        P(),
        P("feat"),
        P(None, "feat"),
        P("feat"),
    )
    return jax.shard_map(
        functools.partial(local, mesh.shape["feat"], RING_X), mesh=mesh, in_specs=placed,
        out_specs=P("node", "feat"), check_vma=False,
    )
```

```python
import functools

import jax
import jax.numpy as jnp
from jax import lax
from jax.experimental import pallas as pl
from jax.experimental.pallas import tpu as pltpu
from jax.sharding import PartitionSpec as P

FAN = 25
RING_X = 4
UNROLL = 4
F32 = jnp.float32
BF16 = jnp.bfloat16
PARTIAL = BF16
EARLY = 4
MESH = pl.DeviceIdType.MESH
NT = (((1,), (1,)), ((), ()))
TN = (((0,), (0,)), ((), ()))


def lists(ring_z):
    far = (ring_z // 2 - 1) // 2
    return far, ring_z // 2 - 1 - far


def pair_up(numbers):
    size = numbers.shape[1] // 2
    return numbers[:, :size] + lax.shift_left(numbers[:, size:], 16)


def take_apart(pairs):
    return jnp.concatenate([lax.bitwise_and(pairs, 0xFFFF), lax.shift_right_logical(pairs, 16)], axis=1)


def kernel(
    sizes,
    feat_hbm, req_hbm, nbr_hbm, tgt_hbm, ws_ref, wn_ref, b1_hbm, w2_hbm, b2_hbm,
    out_ref,
    feat_ref, req_ref, nbr_ref, tgt_ref, b1_ref, w2_ref, b2_ref,
    table, req_out, far_req, near_req, far_out, far_in, near_out, near_in, far_count, near_count,
    nbr_send, nbr_in, his, los, far_sum, near_sum, far_send, opposite_sum,
    w_own, w_nbr, w2_all, bias_out, bias_in, own_out, own_in, mean_out, mean_in, pre_own, y_out, y_in,
    req_ss, far_req_rs, near_req_rs, far_ss, far_rs, near_ss, near_rs, pair_ss, pair_rs,
    in_sem, w_sem, up_ss, up_rs, down_ss, down_rs, on_ss, on_rs, group_ss, group_rs,
):
    ring_x, ring_z, groups, own_rows, targets, cols = sizes
    nodes, chips = ring_x * ring_z, groups // 2
    blocks, part = own_rows // 256, targets // groups // 2
    hidden = groups * 64
    node, feat = lax.axis_index("node"), lax.axis_index("feat")
    my_x, my_z = lax.div(node, ring_z), lax.rem(node, ring_z)
    core = lax.bitwise_and(feat, 1)
    chip = lax.shift_right_logical(feat, 1)
    half = ring_z // 2
    far_reach, near_reach = lists(ring_z)
    far_steps, near_steps = 2 * far_reach + 1, 2 * near_reach + 1
    far_all, near_all = far_steps * ring_x, near_steps * ring_x
    far_self, near_self = far_all - ring_x, near_all - ring_x

    def at(dx, dz):
        z = my_z + dz
        z = jnp.where(z < 0, z + ring_z, jnp.where(z >= ring_z, z - ring_z, z))
        return lax.bitwise_and(my_x + ring_x + dx, ring_x - 1) * ring_z + z

    def place(p, steps):
        if isinstance(p, int):
            step = steps - 1 - p // ring_x
            return p % ring_x, (step + 1) // 2 * (1 if step % 2 else -1)
        step = steps - 1 - lax.shift_right_logical(p, ring_x.bit_length() - 1)
        ahead = lax.shift_right_logical(step + 1, 1)
        return lax.bitwise_and(p, ring_x - 1), jnp.where(lax.bitwise_and(step, 1) == 1, ahead, -ahead)

    def mate(k):
        return lax.bitwise_and(feat + k, groups - 1)

    def copy_to(axis, peer, src, dst, ss, rs):
        return pltpu.make_async_remote_copy(
            src_ref=src, dst_ref=dst, send_sem=ss, recv_sem=rs,
            device_id={axis: peer}, device_id_type=MESH,
        )

    def loop(low, high, body):
        def step(k, carry):
            body(k)
            return carry

        lax.fori_loop(low, high, step, 0)

    arrivals = [
        pltpu.make_async_copy(src, dst, in_sem.at[i])
        for i, (src, dst) in enumerate((
            (req_hbm, req_ref), (nbr_hbm, nbr_ref), (feat_hbm, feat_ref), (w2_hbm, w2_ref),
            (tgt_hbm, tgt_ref), (b1_hbm, b1_ref), (b2_hbm, b2_ref)))]
    for copy in arrivals:
        copy.start()

    barrier = pltpu.get_barrier_semaphore()
    for dz in sorted(range(ring_z), key=lambda z: -min(z, ring_z - z)):
        for dx in range(ring_x):
            if dx or dz:
                pl.semaphore_signal(barrier, inc=1, device_id={"node": at(dx, dz)}, device_id_type=MESH)
    for k in range(1, groups):
        pl.semaphore_signal(barrier, inc=1, device_id={"feat": mate(k)}, device_id_type=MESH)

    w_copies = [
        pltpu.make_async_copy(src, dst.at[:, :, pl.ds(0, cols), :], w_sem.at[i])
        for i, (src, dst) in enumerate(((ws_ref, w_own), (wn_ref, w_nbr)))]
    arrivals[0].wait()
    asked = pair_up(req_ref[...])
    for j in range(nodes):
        req_out[j] = asked[j:j + 1]
    for copy in arrivals[1:]:
        copy.wait()
    nbr_send[...] = pair_up(nbr_ref[...])

    spread = jnp.where(
        lax.bitwise_and(lax.broadcasted_iota(jnp.int32, (FAN, 256), 1), 31)
        == lax.broadcasted_iota(jnp.int32, (FAN, 256), 0), 1.0, 0.0).astype(BF16)

    def spread_slots(slots, which):
        hi = lax.shift_right_logical(slots, 8).astype(F32).astype(BF16)
        lo = lax.bitwise_and(slots, 255).astype(F32).astype(BF16)
        his[which] = lax.dot_general(hi, spread, TN, preferred_element_type=F32)
        los[which] = lax.dot_general(lo, spread, TN, preferred_element_type=F32)

    def count_eight(which, owners, first):
        lane = lax.broadcasted_iota(jnp.int32, (8, 256), 1)
        sub = lax.broadcasted_iota(jnp.int32, (8, 256), 0)
        mine = (lax.shift_right_logical(lane, 5) == sub) & (lax.bitwise_and(lane, 31) < FAN)
        rows = pl.ds(pl.multiple_of(first, 8), 8)
        hi = jnp.where(mine, his[which, rows, :], -1.0)
        lo = jnp.sum(jnp.where(mine, los[which, rows, :], 0.0), axis=0, keepdims=True)
        left = jnp.concatenate([jnp.where(hi == owner, 1.0, 0.0) for owner in owners], axis=0)
        row = lax.broadcasted_iota(jnp.int32, (256, 256), 0)
        right = jnp.where(row == lo.astype(jnp.int32), 1.0, 0.0)
        both = lax.dot_general(left.astype(BF16), right.astype(BF16), NT, preferred_element_type=F32)
        return both.reshape(len(owners), 8, 256)

    def count_some(which, count, steps, low, high):
        owners = []
        for p in range(steps * ring_x):
            dx, dz = place(p, steps)
            owners.append(at(-dx, -dz).astype(F32))

        def body(k):
            for turn in range(UNROLL):
                first = pl.multiple_of((k * UNROLL + turn) * 16, 16)
                both = [count_eight(which, owners, first + 8 * i) for i in range(2)]
                count[:, pl.ds(first, 16), :] = jnp.concatenate(both, axis=1).astype(BF16)

        loop(low, high, body)

    turns = targets // (16 * UNROLL)
    early = min(EARLY, turns)
    spread_slots(nbr_ref[...], 0)
    count_some(0, near_count, near_steps, 0, early)

    pl.semaphore_wait(barrier, nodes - 1 + groups - 1)

    opposite = at(0, half)
    nbr_copy = copy_to("node", opposite, nbr_send, nbr_in, pair_ss.at[0], pair_rs.at[0])
    sum_copy = copy_to("node", opposite, far_send, opposite_sum, pair_ss.at[1], pair_rs.at[1])
    for p in range(far_all):
        dx, dz = place(p, far_steps)
        owner = at(-dx, half - dz)
        copy_to("node", owner, req_out.at[owner], far_req.at[p], req_ss, far_req_rs.at[p // ring_x]).start()
    for p in range(near_all):
        if p != near_self:
            dx, dz = place(p, near_steps)
            owner = at(-dx, -dz)
            copy_to("node", owner, req_out.at[owner], near_req.at[p], req_ss, near_req_rs.at[p // ring_x]).start()
    near_req[near_self] = req_out[node]
    nbr_copy.start()

    for copy in w_copies:
        copy.start()
    for j in range(blocks):
        table[pl.ds(j * cols, cols), :] = feat_ref[:, pl.ds(j * 256, 256)]
    bias_out[...] = jnp.zeros_like(bias_out)
    bias_out[pl.ds(0, 1), pl.ds(0, 64)] = b1_ref[...]
    bias_out[pl.ds(1, 1), pl.ds(0, 64)] = b2_ref[...]
    bias_out[...] = bias_out[...] + pltpu.roll(bias_out[...], 64, 1)
    bias_in[0] = bias_out[...]

    ups, downs = chips // 2, (chips - 1) // 2

    def up(step):
        slot = w2_all.at[core, lax.bitwise_and(chip - step + chips, chips - 1)]
        return copy_to("feat", mate(2), slot if step else w2_ref, slot, up_ss.at[step], up_rs.at[step])

    def down(step):
        slot = w2_all.at[core, lax.bitwise_and(chip + step, chips - 1)]
        return copy_to("feat", mate(groups - 2), slot if step else w2_ref, slot, down_ss.at[step], down_rs.at[step])

    def pass_on(step):
        for copy, steps in ((up, ups), (down, downs)):
            if 0 < step <= steps:
                copy(step - 1).wait_recv()
            if step < steps:
                copy(step).start()

    w2_all[core, chip] = w2_ref[...]
    pass_on(0)

    def to_mates(src, dst, which):
        for k in sorted(range(1, groups), key=lambda k: -min(k, groups - k)):
            peer = mate(k)
            copy_to("feat", peer, src(peer), dst.at[k], group_ss.at[which], group_rs.at[which]).start()

    def from_mates(dst, which):
        rest = dst.at[pl.ds(1, groups - 1)]
        return copy_to("feat", mate(1), rest, rest, group_ss.at[which], group_rs.at[which])

    def pick(index):
        block, within = lax.shift_right_logical(index, 8), lax.bitwise_and(index, 255)
        row = lax.broadcasted_iota(jnp.int32, (256, 256), 0)
        one_hot = jnp.where(row == within, 1.0, 0.0).astype(BF16)
        every = jnp.dot(table[...], one_hot, preferred_element_type=F32)
        found = every[0:cols]
        for j in range(1, blocks):
            found = jnp.where(block == j, every[j * cols:(j + 1) * cols], found)
        return found

    def span(refs, first, size):
        return refs.at[pl.ds(first, size)]

    def arrive(refs, sems, first, size, group):
        rest = span(refs, first, size)
        copy_to("node", opposite, rest, rest, req_ss, sems.at[group]).wait_recv()

    def serve(req, req_rs, out, into, ss, rs, steps, group, entries):
        arrive(req, req_rs, entries[0], len(entries), group)
        for p in entries:
            out[p] = pick(take_apart(req[p])).astype(BF16)
        for p in entries:
            dx, dz = place(p, steps)
            copy_to("node", at(dx, dz), out.at[p], into.at[p], ss, rs.at[group]).start()

    loop(0, far_steps - 1, lambda g: serve(
        far_req, far_req_rs, far_out, far_in, far_ss, far_rs, far_steps, g,
        [ring_x * g + j for j in range(ring_x)]))
    arrive(far_req, far_req_rs, far_self, ring_x, far_steps - 1)
    for p in range(far_self, far_all):
        found = pick(take_apart(far_req[p])).astype(BF16)
        if p == far_self:
            far_in[p] = found
        else:
            far_out[p] = found
            dx, dz = place(p, far_steps)
            copy_to("node", at(dx, dz), far_out.at[p], far_in.at[p], far_ss, far_rs.at[far_steps - 1]).start()
    pass_on(1)
    loop(0, near_steps - 1, lambda g: serve(
        near_req, near_req_rs, near_out, near_in, near_ss, near_rs, near_steps, g,
        [ring_x * g + j for j in range(ring_x)]))
    serve(near_req, near_req_rs, near_out, near_in, near_ss, near_rs, near_steps, near_steps - 1,
          list(range(near_self + 1, near_all)))
    near_in[near_self] = pick(take_apart(near_req[near_self])).astype(BF16)
    pass_on(2)

    nbr_copy.wait_recv()
    spread_slots(take_apart(nbr_in[...]), 1)
    count_some(1, far_count, far_steps, 0, turns)

    def add_rows(total, count, rows, entries):
        for p in entries:
            total = total + lax.dot_general(rows[p], count[p], NT, preferred_element_type=F32)
        return total

    def take(rows, rs, count, sums, group, entries):
        arrive(rows, rs, entries[0], len(entries), group)
        sums[...] = add_rows(sums[...], count, rows, entries)

    def take_all(rows, rs, count, sums, steps):
        own = (steps - 1) * ring_x
        sums[...] = add_rows(jnp.zeros_like(sums), count, rows, [own])
        loop(0, steps - 1, lambda g: take(rows, rs, count, sums, g, [ring_x * g + j for j in range(ring_x)]))
        take(rows, rs, count, sums, steps - 1, list(range(own + 1, own + ring_x)))

    take_all(far_in, far_rs, far_count, far_sum, far_steps)
    far_send[...] = far_sum[...].astype(PARTIAL)
    sum_copy.start()
    pass_on(3)

    def pack(turned):
        gap = jnp.zeros((64 - cols, targets // 2), F32)
        return jnp.concatenate(
            [turned[:, :targets // 2], gap, turned[:, targets // 2:], gap], axis=0).T.astype(BF16)

    def share_of(ref):
        return lambda peer: ref.at[pl.ds(pl.multiple_of(peer * part, part), part), :]

    low_half = lax.broadcasted_iota(jnp.int32, (1, 128), 1) < 64

    def unpack(ref):
        tiles = [ref[lax.bitwise_and(feat - j + groups, groups - 1)].astype(F32) for j in range(groups)]
        tops, bottoms = [], []
        for left, right in zip(tiles[::2], tiles[1::2], strict=True):
            tops.append(jnp.where(low_half, left, pltpu.roll(right, 64, 1)).astype(BF16))
            bottoms.append(jnp.where(low_half, pltpu.roll(left, 64, 1), right).astype(BF16))
        return jnp.concatenate([jnp.concatenate(tops, axis=1), jnp.concatenate(bottoms, axis=1)], axis=0)

    own = jnp.concatenate([pick(tgt_ref[:, pl.ds(j * 256, 256)]) for j in range(targets // 256)], axis=1)
    own_out[...] = pack(own)
    own_in[0] = own_out[pl.ds(pl.multiple_of(feat * part, part), part), :]
    to_mates(share_of(own_out), own_in, 0)
    to_mates(lambda peer: bias_out, bias_in, 1)

    count_some(0, near_count, near_steps, early, turns)
    pass_on(4)
    side = copy_to("feat", feat + 1 - 2 * core, w2_all.at[core], w2_all.at[core], on_ss, on_rs)
    side.start()

    for copy, weight in zip(w_copies, (w_own, w_nbr), strict=True):
        weight[:, :, pl.ds(cols, 64 - cols), :] = jnp.zeros((chips, 2, 64 - cols, hidden), BF16)
        copy.wait()
    from_mates(own_in, 0).wait_recv()
    from_mates(bias_in, 1).wait_recv()

    def bias_row(row, order):
        def of(g):
            return bias_in[lax.bitwise_and(feat - g + groups, groups - 1), pl.ds(row, 1), :]

        pairs = zip(order[::2], order[1::2], strict=True)
        return jnp.concatenate([jnp.where(low_half, of(a), of(b)) for a, b in pairs], axis=1)

    by_core = [2 * j + c for c in range(2) for j in range(chips)]
    second_bias = bias_row(1, by_core)
    pre_own[...] = jnp.dot(
        unpack(own_in), w_own[...].reshape(groups * 64, hidden), preferred_element_type=F32,
    ) + bias_row(0, list(range(groups)))

    take_all(near_in, near_rs, near_count, near_sum, near_steps)

    def sent(refs, size, sem):
        rest = span(refs, 0, size)
        copy_to("node", opposite, rest, rest, sem, pair_rs.at[0]).wait_send()

    sent(req_out, nodes - 1, req_ss)
    sent(far_out, far_all - 1, far_ss)
    nbr_copy.wait_send()
    for copy, steps in ((up, ups), (down, downs)):
        for step in range(steps):
            copy(step).wait_send()
    from_mates(own_in, 0).wait_send()
    from_mates(bias_in, 1).wait_send()

    sum_copy.wait_recv()
    mean_out[...] = pack((near_sum[...] + opposite_sum[...].astype(F32)) / FAN)
    to_mates(share_of(mean_out), mean_in, 2)
    mean_in[0] = mean_out[pl.ds(pl.multiple_of(feat * part, part), part), :]
    sum_copy.wait_send()
    sent(near_out, near_all - 1, near_ss)
    side.wait_send()
    other = w2_all.at[1 - core]
    copy_to("feat", feat + 1 - 2 * core, other, other, on_ss, on_rs).wait_recv()
    from_mates(mean_in, 2).wait_recv()

    pre = pre_own[...] + jnp.dot(
        unpack(mean_in), w_nbr[...].reshape(groups * 64, hidden), preferred_element_type=F32)
    one = jnp.maximum(pre, 0.0).astype(BF16)
    two = lax.dot_general(one, w2_all[...].reshape(hidden, hidden), NT, preferred_element_type=F32) + second_bias
    for j in range(groups // 2):
        above, below = two[:part, j * 128:(j + 1) * 128], two[part:, j * 128:(j + 1) * 128]
        y_out[2 * j] = jnp.where(low_half, above, pltpu.roll(below, 64, 1)).astype(BF16)
        y_out[2 * j + 1] = jnp.where(low_half, pltpu.roll(above, 64, 1), below).astype(BF16)

    def rank(peer):
        return lax.bitwise_and(peer, 1) * chips + lax.shift_right_logical(peer, 1)

    to_mates(lambda peer: y_out.at[rank(peer)], y_in, 3)
    y_in[0] = y_out[rank(feat)]
    from_mates(mean_in, 2).wait_send()
    from_mates(y_in, 3).wait_recv()
    shares = [y_in[lax.bitwise_and(feat - j + groups, groups - 1)] for j in range(groups)]
    turned = jnp.concatenate(shares, axis=0).astype(F32).T
    out_ref[...] = jnp.concatenate([turned[0:64], turned[64:128]], axis=1).astype(BF16)
    from_mates(y_in, 3).wait_send()


def local(groups, ring_x, features, req_local, nbr_slot, target_ids, w_self, w_neigh, bias_one, w_two, bias_two):
    _, nodes, cap = req_local.shape
    own_rows, cols = features.shape
    targets, fan = nbr_slot.shape
    hidden = w_self.shape[1]
    part, chips = targets // groups // 2, groups // 2
    sizes = (ring_x, nodes // ring_x, groups, own_rows, targets, cols)
    far_steps, near_steps = (2 * reach + 1 for reach in lists(nodes // ring_x))
    far, near = far_steps * ring_x, near_steps * ring_x
    vmem = pl.BlockSpec(memory_space=pltpu.VMEM)
    hbm = pl.BlockSpec(memory_space=pl.ANY)
    dma = pltpu.SemaphoreType.DMA
    out = pl.pallas_call(
        functools.partial(kernel, sizes),
        out_shape=jax.ShapeDtypeStruct((64, targets), BF16),
        in_specs=[hbm] * 9,
        out_specs=vmem,
        scratch_shapes=[
            pltpu.VMEM((cols, own_rows), BF16),
            pltpu.VMEM((nodes, cap), jnp.int32),
            pltpu.VMEM((fan, targets), jnp.int32),
            pltpu.VMEM((1, targets), jnp.int32),
            pltpu.VMEM((1, 64), F32),
            pltpu.VMEM((64, hidden), BF16),
            pltpu.VMEM((1, 64), F32),
            pltpu.VMEM((own_rows // 256 * cols, 256), BF16),
            pltpu.VMEM((nodes, 1, cap // 2), jnp.int32),
            pltpu.VMEM((far, 1, cap // 2), jnp.int32),
            pltpu.VMEM((near, 1, cap // 2), jnp.int32),
            pltpu.VMEM((far, cols, cap), BF16),
            pltpu.VMEM((far, cols, cap), BF16),
            pltpu.VMEM((near, cols, cap), BF16),
            pltpu.VMEM((near, cols, cap), BF16),
            pltpu.VMEM((far, targets, cap), BF16),
            pltpu.VMEM((near, targets, cap), BF16),
            pltpu.VMEM((fan, targets // 2), jnp.int32),
            pltpu.VMEM((fan, targets // 2), jnp.int32),
            pltpu.VMEM((2, targets, 256), F32),
            pltpu.VMEM((2, targets, 256), F32),
            pltpu.VMEM((cols, targets), F32),
            pltpu.VMEM((cols, targets), F32),
            pltpu.VMEM((cols, targets), PARTIAL),
            pltpu.VMEM((cols, targets), PARTIAL),
            pltpu.VMEM((chips, 2, 64, hidden), BF16),
            pltpu.VMEM((chips, 2, 64, hidden), BF16),
            pltpu.VMEM((2, chips, 64, hidden), BF16),
            pltpu.VMEM((8, 128), F32),
            pltpu.VMEM((groups, 8, 128), F32),
            pltpu.VMEM((targets // 2, 128), BF16),
            pltpu.VMEM((groups, part, 128), BF16),
            pltpu.VMEM((targets // 2, 128), BF16),
            pltpu.VMEM((groups, part, 128), BF16),
            pltpu.VMEM((2 * part, hidden), F32),
            pltpu.VMEM((groups, part, 128), BF16),
            pltpu.VMEM((groups, part, 128), BF16),
            dma(()), dma((far_steps,)), dma((near_steps,)),
            dma(()), dma((far_steps,)), dma(()), dma((near_steps,)), dma((2,)), dma((2,)),
            dma((7,)), dma((2,)), dma((4,)), dma((4,)), dma((4,)), dma((4,)), dma(()), dma(()), dma((4,)), dma((4,)),
        ],
        compiler_params=pltpu.CompilerParams(
            collective_id=0, has_side_effects=True, vmem_limit_bytes=56 * 1024 * 1024
        ),
    )(
        features.T, req_local[0], nbr_slot.T, target_ids[None, :],
        w_self.reshape(chips, 2, cols, hidden), w_neigh.reshape(chips, 2, cols, hidden),
        bias_one[None, :], w_two.T, bias_two[None, :],
    )
    return out.T


def solution(mesh):
    placed = (
        P("node", "feat"),
        P("node", None, None),
        P("node", None),
        P("node"),
        P(),
        P(),
        P("feat"),
        P(None, "feat"),
        P("feat"),
    )
    return jax.shard_map(
        functools.partial(local, mesh.shape["feat"], RING_X), mesh=mesh, in_specs=placed,
        out_specs=P("node", "feat"), check_vma=False,
    )
```
